32 devices in a mesh: ha: 2 (over y), az: 16 (over z, x, core).
Axes of the slice: x: 2, y: 2, z: 4, core: 2. Of those that a mesh axis runs over, the one named last changes fastest.
Arguments:
- field: float32 [2, 4096, 8192], P(None, 'ha', 'az'), may hold values from -6 to 6
- terrain: int32 [8192], P('az'), may hold values from 0 to 63
- profile_pick: int32 [8192], P('az'), may hold values from 0 to 15
- profile_table: float32 [16, 4096], replicated, may hold values from -3.140625 to 3.140625
- clutter_mask: int32 [128, 8192], P(None, 'az'), may hold values 0 or 1
- pulse: float32 [63], replicated, may hold values from -0.6 to 0.6
- beam: float32 [31], replicated, may hold values from -0.9 to 0.9
- measured: float32 [2, 128, 8192], P(None, None, 'az'), may hold values from -6 to 6
Outputs:
- field_out: float32 [2, 4096, 8192], P(None, 'ha', 'az')
- sources: float32 [2, 2, 128, 8192], P(None, None, 'ha', 'az')
The draws below stay inside these ranges and needn't reach their ends.
All inputs are finite; a program needn't handle non-finite values. No bound on the sum of `clutter_mask` on one device may be relied on, other than what follows from the above.
Results may differ from the reference program's by a relative error of at most 0.00022.
Values sent between devices are 32-bit elements; how exact they have to be, the bound alone decides.
A program may use at most 128 MiB of HBM per device.

```python
import math
import jax
import jax.numpy as jnp
from jax import lax

NH = 4096
NA = 8192
BOT = 128
RTAPS = 63
ATAPS = 31
NPROF = 16
STEPS = 2


def plant(values, own_key, low, largest):
    spot = [jax.random.randint(jax.random.fold_in(own_key, axis), (), 0, length) for axis, length in enumerate(values.shape)]
    widest = values.shape.index(max(values.shape))
    beside = spot[:widest] + [(spot[widest] + 1) % values.shape[widest]] + spot[widest + 1:]
    return values.at[tuple(spot)].set(low).at[tuple(beside)].set(largest)


def shard_levels(stream_key, shape, pieces, low, high):
    level = 1.0
    for position, blocks in pieces:
        steps = jax.random.uniform(jax.random.fold_in(jax.random.fold_in(stream_key, 6), position), (blocks,), jnp.float32, low / len(pieces), high / len(pieces))
        level = level * jnp.repeat(jnp.exp(steps), shape[position] // blocks).reshape((-1,) + (1,) * (len(shape) - 1 - position))
    return level


def normal_values(key, shape, width, limit, cuts=(), held_as=jnp.bfloat16):
    values = width * jax.random.normal(key, shape, jnp.float32)
    if cuts:
        values = values * shard_levels(key, shape, cuts, -0.22, 0.18)
    return jnp.clip(values, -limit, limit).astype(held_as)


def setup_inputs(seed: int = 0) -> dict:
    streams_of = jax.random.split(jax.random.key(seed), 9)
    return {
        "field": normal_values(streams_of[0], (2, NH, NA), 1.0, 6.0, ((1, 2), (2, 16)), jnp.float32),
        "terrain": plant(jax.random.randint(streams_of[1], (NA,), 0, BOT // 2), jax.random.fold_in(streams_of[1], 1), 0, (BOT // 2) - 1).astype(jnp.int32),
        "profile_pick": plant(jax.random.randint(streams_of[2], (NA,), 0, NPROF), jax.random.fold_in(streams_of[2], 1), 0, NPROF - 1).astype(jnp.int32),
        "profile_table": jnp.clip(jax.random.uniform(streams_of[3], (NPROF, NH), jnp.float32, -3.140625, 3.140625), -3.140625, 3.140625),
        "clutter_mask": plant((jax.random.randint(streams_of[4], (BOT, NA), 0, 4) < 3).astype(jnp.int32), jax.random.fold_in(streams_of[4], 1), 0, 1),
        "pulse": normal_values(streams_of[5], (RTAPS,), 0.126, 0.6, (), jnp.float32),
        "beam": normal_values(streams_of[6], (ATAPS,), 0.18, 0.9, (), jnp.float32),
        "measured": normal_values(streams_of[7], (STEPS, BOT, NA), 1.0, 6.0, ((2, 16),), jnp.float32),
    }


height_chirp = 1
azimuth_chirp = 3


def chirp_angle(count, spread):
    index = jnp.arange(count, dtype=jnp.int32)
    return ((spread * index * index) % (2 * count)).astype(jnp.float32) * (-math.pi / count)


def screen_coef(rows, terr, phase, total):
    height = rows.astype(jnp.float32)
    depth = jnp.maximum(height - 0.75 * total, 0.0) / (0.25 * total)
    amount = jnp.exp(-4.0 * depth * depth) * (rows >= terr).astype(jnp.float32)
    return amount * jnp.cos(phase), amount * jnp.sin(phase)


def range_band(pulse, bottom):
    taps = pulse.shape[0]
    half = (taps - 1) // 2
    row = lax.broadcasted_iota(jnp.int32, (bottom, bottom), 0)
    col = lax.broadcasted_iota(jnp.int32, (bottom, bottom), 1)
    offset = col - row + half
    hit = offset[:, :, None] == jnp.arange(taps, dtype=jnp.int32)[None, None, :]
    return jnp.sum(jnp.where(hit, pulse[None, None, :], 0.0), axis=-1)


def reference(field, terrain, profile_pick, profile_table, clutter_mask, pulse, beam, measured):
    highest = lax.Precision.HIGHEST
    rows = jnp.arange(NH, dtype=jnp.int32)[:, None]
    phase = jnp.take(profile_table, profile_pick, axis=0).T
    coef_re, coef_im = screen_coef(rows, terrain[None, :], phase, NH)
    coef = coef_re + 1j * coef_im
    angle_z = chirp_angle(NH, height_chirp)
    angle_y = chirp_angle(NA, azimuth_chirp)
    kern_z = jnp.cos(angle_z) + 1j * jnp.sin(angle_z)
    kern_y = jnp.cos(angle_y) + 1j * jnp.sin(angle_y)
    mask = clutter_mask.astype(jnp.float32)
    rmat = range_band(pulse, BOT)
    half_beam = (ATAPS - 1) // 2
    wave = field[0] + 1j * field[1]
    result = []
    for step in range(STEPS):
        wave = jnp.fft.ifft(jnp.fft.fft(wave, axis=1) * kern_y[None, :], axis=1)
        wave = jnp.fft.ifft(jnp.fft.fft(wave, axis=0) * kern_z[:, None], axis=0)
        wave = wave * coef
        low_re = jnp.real(wave[:BOT])
        low_im = jnp.imag(wave[:BOT])
        power = mask * (low_re * low_re + low_im * low_im)
        ranged = jnp.dot(rmat, power, precision=highest)
        model = jnp.zeros_like(ranged)
        for tap in range(ATAPS):
            model = model + beam[tap] * jnp.roll(ranged, half_beam - tap, axis=1)
        misfit = model - measured[step]
        spread_back = jnp.zeros_like(misfit)
        for tap in range(ATAPS):
            spread_back = spread_back + beam[tap] * jnp.roll(misfit, tap - half_beam, axis=1)
        back = jnp.dot(rmat.T, spread_back, precision=highest)
        result.append(jnp.stack([2.0 * mask * low_re * back, 2.0 * mask * low_im * back]))
    field_out = jnp.stack([jnp.real(wave), jnp.imag(wave)])
    return field_out, jnp.stack(result)
```

```python
import math

import jax
import jax.numpy as jnp
import numpy as np
from jax import lax
from jax.sharding import PartitionSpec as P

height_chirp = 1
azimuth_chirp = 3
EXACT = lax.Precision.HIGHEST
FAST = lax.Precision.HIGH


def iota(shape, dim):
    return lax.broadcasted_iota(jnp.int32, shape, dim)


def cmul(left, right):
    return (left[0] * right[0] - left[1] * right[1], left[0] * right[1] + left[1] * right[0])


def turn(amount, period, scale=1.0):
    angle = (amount % period).astype(jnp.float32) * (2.0 * math.pi / period)
    return (scale * jnp.cos(angle), scale * jnp.sin(angle))


def inverse_of(spread, count):
    return pow(spread, -1, 2 * count)


def gauss(spread, count):
    index = np.arange(count, dtype=np.int64)
    angle = (spread * index * index % (2 * count)) * (-math.pi / count)
    return (float(np.sum(np.cos(angle))) / count, float(np.sum(np.sin(angle))) / count)


def chirp(index, spread, count):
    return turn(index * index % (2 * count) * inverse_of(spread, count), 2 * count)


def roots(size, spread, count):
    amount = iota((size, size), 0) * iota((size, size), 1) % size * (inverse_of(spread, count) % size)
    re, im = turn(-amount, size)
    return jnp.stack([jnp.stack([re, -im]), jnp.stack([im, re])])


def twist(rows, cols, spread, count):
    left, right = iota((rows, cols), 0), iota((rows, cols), 1)
    return turn(-(left * right % count * (inverse_of(spread, count) % count)), count)


def band(taps, offset):
    hit = offset[:, :, None] == lax.broadcasted_iota(jnp.int32, (1, 1, taps.shape[0]), 2)
    return jnp.sum(jnp.where(hit, taps[None, None, :], 0.0), axis=-1)


def damping(rows, total):
    depth = jnp.maximum(rows.astype(jnp.float32) - 0.75 * total, 0.0) / (0.25 * total)
    return jnp.exp(-4.0 * depth * depth)


def onehot_of(picks, count):
    return (picks[None] == iota((count,) + picks.shape, 0)).astype(jnp.float32)


def halo(cells, width, axis="az"):
    count = lax.axis_size(axis)
    head = cells[..., :width]
    tail = cells[..., cells.shape[-1] - width:]
    left = lax.ppermute(tail, axis, [(i, (i + 1) % count) for i in range(count)])
    right = lax.ppermute(head, axis, [((i + 1) % count, i) for i in range(count)])
    return left, right


def local(field, terrain, profile_pick, profile_table, clutter_mask, pulse, beam, measured):
    n_ha = lax.axis_size("ha")
    n_az = lax.axis_size("az")
    n_dev = n_ha * n_az
    slab = lax.axis_index("ha")
    block = lax.axis_index("az")
    place = block * n_ha + slab
    both = ("az", "ha")
    h_dev, a_dev = field.shape[1], field.shape[2]
    total_h, total_a = h_dev * n_ha, a_dev * n_az
    cols = a_dev // n_ha
    bottom = clutter_mask.shape[0]
    h_first = max(64, n_dev)
    h_second = total_h // h_first
    own = h_first // n_dev
    n_prof = profile_table.shape[0]

    taps_range = pulse.shape[0]
    half_range = (taps_range - 1) // 2
    half_beam = (beam.shape[0] - 1) // 2
    reach = 2 * half_beam
    wide = a_dev + 2 * reach
    middle = a_dev + 2 * half_beam
    share = bottom // n_ha
    rmat = band(pulse, iota((bottom, bottom), 1) - iota((bottom, bottom), 0) + half_range)
    forward_band = band(beam, iota((wide, middle), 0) - iota((wide, middle), 1))
    back_band = band(beam, iota((middle, a_dev), 1) - iota((middle, a_dev), 0) + reach)
    own_rmat = lax.dynamic_slice_in_dim(rmat, slab * share, share, 1)
    mask = clutter_mask.astype(jnp.float32)
    left, right = halo(mask, reach)
    wide_mask = jnp.concatenate([left, mask, right], axis=1)
    left, right = halo(measured, half_beam)
    wide_measured = jnp.concatenate([left, measured, right], axis=2)

    def sources_of(low_re, low_im, step):
        power = wide_mask * (low_re * low_re + low_im * low_im)
        ranged = jnp.dot(rmat, power, precision=EXACT)
        misfit = jnp.dot(ranged, forward_band, precision=EXACT) - wide_measured[step]
        spread_back = jnp.dot(misfit, back_band, precision=EXACT)
        back = jnp.einsum("pr,pa->ra", own_rmat, spread_back, precision=EXACT)
        weight = 2.0 * lax.dynamic_slice_in_dim(mask, slab * share, share, 0) * back
        mine = [
            lax.dynamic_slice(low, (slab * share, reach), (share, a_dev)) for low in (low_re, low_im)
        ]
        return jnp.stack([weight * mine[0], weight * mine[1]])

    all_pick = lax.all_gather(profile_pick, "az", tiled=True)
    all_terrain = lax.all_gather(terrain, "az", tiled=True)
    height = iota((1, total_h), 1)
    z_chirp = chirp(height, height_chirp, total_h)
    z_gain = gauss(height_chirp, total_h)
    y_gain = gauss(azimuth_chirp, total_a)
    gain = (z_gain[0] * y_gain[0] - z_gain[1] * y_gain[1], z_gain[0] * y_gain[1] + z_gain[1] * y_gain[0])
    amount = damping(height, total_h)
    bend = cmul((amount * jnp.cos(profile_table), amount * jnp.sin(profile_table)), cmul(z_chirp, gain))
    bend_again = cmul(bend, z_chirp)

    slab_z = chirp(slab * h_dev + iota((h_dev, 1), 0), height_chirp, total_h)
    block_y = chirp(block * a_dev + iota((1, a_dev), 1), azimuth_chirp, total_a)
    start = cmul((field[0], field[1]), cmul(slab_z, block_y))
    start = jnp.stack(start).reshape(2, h_dev, n_ha, cols).transpose(2, 0, 1, 3)

    w_first = roots(h_first, height_chirp, total_h)
    w_second = roots(h_second, height_chirp, total_h)
    tw_re, tw_im = (t[:, :, None] for t in twist(h_first, h_second, height_chirp, total_h))
    tall = lax.all_to_all(start, "ha", split_axis=0, concat_axis=0)
    tall = tall.reshape(n_ha, 2, h_first // n_ha, h_second, cols)
    w_in = w_first.reshape(2, 2, h_first, n_ha, h_first // n_ha)
    tall = jnp.einsum("ocksa,scabq->okbq", w_in, tall, precision=FAST)
    tall = jnp.stack(cmul(tall, (tw_re, tw_im)))
    tall = jnp.einsum("ocjb,ckbq->kojq", w_second, tall, precision=FAST)
    tall = tall.reshape(n_dev, own, 2, h_second, cols)
    rows = lax.all_to_all(tall, both, split_axis=0, concat_axis=0)

    w_blocks = roots(n_dev, azimuth_chirp, total_a)
    w_cols = roots(cols, azimuth_chirp, total_a)
    ty_re, ty_im = (t[:, None, None, :] for t in twist(n_dev, cols, azimuth_chirp, total_a))
    rows = jnp.einsum("ocnp,pucjq->onujq", w_blocks, rows, precision=FAST)
    rows = jnp.stack(cmul(rows, (ty_re, ty_im)))
    rows = jnp.einsum("ocmq,cnujq->onujm", w_cols, rows, precision=FAST)

    def own_rows(table):
        table = table.reshape(n_prof, h_second, n_dev, own)
        table = lax.dynamic_slice_in_dim(table, place, 1, 2)[:, :, 0]
        return jnp.swapaxes(table, 1, 2)

    own_first = place * own + iota((1, own, 1, 1), 1)
    own_height = own_first + h_first * iota((1, 1, h_second, 1), 2)
    grid_pick = all_pick.reshape(cols, n_dev).T
    grid_terrain = all_terrain.reshape(cols, n_dev).T
    hot = onehot_of(grid_pick, n_prof)
    azimuth = iota((n_dev, cols), 0) + n_dev * iota((n_dev, cols), 1)
    y_chirp = chirp(azimuth, azimuth_chirp, total_a)
    ground = (own_height >= grid_terrain[:, None, None, :]).astype(jnp.float32)
    y_turn = tuple(t[:, None, None, :] for t in cmul(y_chirp, y_chirp))
    bent = tuple(
        ground * jnp.einsum("fuj,fnm->nujm", own_rows(t), hot, precision=FAST) for t in bend_again
    )
    next_rows = jnp.stack(cmul(rows, cmul(bent, y_turn)))

    n_low = -(-bottom // h_first)
    low_bend = tuple(
        ground[:, :, :n_low]
        * jnp.einsum("fuj,fnm->nujm", own_rows(t)[:, :, :n_low], hot, precision=EXACT)
        for t in bend
    )
    low_chirp = tuple(t[:, None, None, :] for t in y_chirp)
    low = jnp.stack(cmul(rows[:, :, :, :n_low], cmul(low_bend, low_chirp)))
    low = low.transpose(0, 2, 3, 4, 1).reshape(2, own, n_low, total_a)
    low = jnp.concatenate([low[..., total_a - reach:], low, low[..., :reach]], axis=-1)
    if bottom % h_first == 0:
        windows = jnp.stack([low[..., i * a_dev:i * a_dev + wide] for i in range(n_az)])
        windows = lax.all_to_all(windows, "az", split_axis=0, concat_axis=0)
        windows = lax.all_gather(windows, "ha")
        windows = windows.transpose(2, 4, 1, 0, 3, 5).reshape(2, bottom, wide)
    else:
        spread = jnp.zeros((2, h_first, n_low, low.shape[-1]), jnp.float32)
        spread = lax.dynamic_update_slice_in_dim(spread, low, place * own, 1)
        spread = jnp.swapaxes(spread, 1, 2).reshape(2, n_low * h_first, low.shape[-1])
        spread = lax.psum(spread[:, :bottom], both)
        windows = lax.dynamic_slice_in_dim(spread, block * a_dev, wide, 2)
    first_sources = sources_of(windows[0], windows[1], 0)

    rows = jnp.einsum("ocqm,cnujm->onujq", w_cols, next_rows, precision=FAST)
    rows = jnp.stack(cmul(rows, (ty_re, ty_im)))
    rows = jnp.einsum("ocpn,cnujq->puojq", w_blocks, rows, precision=FAST)
    tall = lax.all_to_all(rows, both, split_axis=0, concat_axis=0)
    tall = tall.reshape(h_first, 2, h_second, cols)
    tall = jnp.einsum("ocbj,kcjq->okbq", w_second, tall, precision=FAST)
    tall = jnp.stack(cmul(tall, (tw_re, tw_im)))
    tall = jnp.einsum("ocak,ckbq->oabq", w_first, tall, precision=FAST)
    tall = tall.reshape(2, total_h, cols)

    col_start = slab * cols
    tall_pick = lax.dynamic_slice_in_dim(profile_pick, col_start, cols, 0)
    tall_terrain = lax.dynamic_slice_in_dim(terrain, col_start, cols, 0)
    tall_hot = onehot_of(tall_pick, n_prof)
    tall_ground = (iota((total_h, 1), 0) >= tall_terrain[None, :]).astype(jnp.float32)
    tall_y = chirp(block * a_dev + col_start + iota((1, cols), 1), azimuth_chirp, total_a)
    tall_bent = tuple(
        tall_ground * jnp.einsum("fh,fq->hq", t, tall_hot, precision=FAST) for t in bend
    )
    last = jnp.stack(cmul(tall, cmul(tall_bent, tall_y)))

    strip = lax.all_gather(last[:, :bottom], "ha", axis=2, tiled=True)
    left, right = halo(strip, reach)
    strip = jnp.concatenate([left, strip, right], axis=2)
    second_sources = sources_of(strip[0], strip[1], 1)

    out = last.reshape(2, n_ha, h_dev, cols).transpose(1, 0, 2, 3)
    out = lax.all_to_all(out, "ha", split_axis=0, concat_axis=0)
    out = out.transpose(1, 2, 0, 3).reshape(2, h_dev, a_dev)
    return (out, jnp.stack([first_sources, second_sources]))


def solution(mesh):
    return jax.shard_map(
        local,
        mesh=mesh,
        in_specs=(
            P(None, "ha", "az"),
            P("az"),
            P("az"),
            P(),
            P(None, "az"),
            P(),
            P(),
            P(None, None, "az"),
        ),
        out_specs=(P(None, "ha", "az"), P(None, None, "ha", "az")),
        check_vma=False,
    )
```

```python
import math

import jax
import jax.numpy as jnp
import numpy as np
from jax import lax
from jax.sharding import PartitionSpec as P

height_chirp = 1
azimuth_chirp = 3
EXACT = lax.Precision.HIGHEST
FAST = lax.Precision.HIGH


def iota(shape, dim):
    return lax.broadcasted_iota(jnp.int32, shape, dim)


def cmul(left, right):
    return (left[0] * right[0] - left[1] * right[1], left[0] * right[1] + left[1] * right[0])


def turn(amount, period, scale=1.0):
    angle = (amount % period).astype(jnp.float32) * (2.0 * math.pi / period)
    return (scale * jnp.cos(angle), scale * jnp.sin(angle))


def inverse_of(spread, count):
    return pow(spread, -1, 2 * count)


def gauss(spread, count):
    index = np.arange(count, dtype=np.int64)
    angle = (spread * index * index % (2 * count)) * (-math.pi / count)
    return (float(np.sum(np.cos(angle))) / count, float(np.sum(np.sin(angle))) / count)


def chirp(index, spread, count):
    return turn(index * index % (2 * count) * inverse_of(spread, count), 2 * count)


def roots(size, spread, count):
    amount = iota((size, size), 0) * iota((size, size), 1) % size * (inverse_of(spread, count) % size)
    re, im = turn(-amount, size)
    return jnp.stack([jnp.stack([re, -im]), jnp.stack([im, re])])


def twist(rows, cols, spread, count):
    left, right = iota((rows, cols), 0), iota((rows, cols), 1)
    return turn(-(left * right % count * (inverse_of(spread, count) % count)), count)


def band(taps, offset):
    hit = offset[:, :, None] == lax.broadcasted_iota(jnp.int32, (1, 1, taps.shape[0]), 2)
    return jnp.sum(jnp.where(hit, taps[None, None, :], 0.0), axis=-1)


def damping(rows, total):
    depth = jnp.maximum(rows.astype(jnp.float32) - 0.75 * total, 0.0) / (0.25 * total)
    return jnp.exp(-4.0 * depth * depth)


def onehot_of(picks, count):
    return (picks[None] == iota((count,) + picks.shape, 0)).astype(jnp.float32)


def halo(cells, width, axis="az"):
    count = lax.axis_size(axis)
    head = cells[..., :width]
    tail = cells[..., cells.shape[-1] - width:]
    left = lax.ppermute(tail, axis, [(i, (i + 1) % count) for i in range(count)])
    right = lax.ppermute(head, axis, [((i + 1) % count, i) for i in range(count)])
    return left, right


def choose(options, index):
    picked = options[0]
    for i in range(1, len(options)):
        picked = jnp.where(index == i, options[i], picked)
    return picked


def ha_trade(piece_for):
    count = lax.axis_size("ha")
    slab = lax.axis_index("ha")
    parts = [piece_for(slab)]
    for shift in range(1, count):
        pairs = [(i, (i + shift) % count) for i in range(count)]
        parts.append(lax.ppermute(piece_for((slab + shift) % count), "ha", pairs))
    return parts


def ha_order(parts):
    count = len(parts)
    slab = lax.axis_index("ha")
    return [choose(parts, (slab - source) % count) for source in range(count)]


def local(field, terrain, profile_pick, profile_table, clutter_mask, pulse, beam, measured):
    n_ha = lax.axis_size("ha")
    n_az = lax.axis_size("az")
    n_dev = n_ha * n_az
    slab = lax.axis_index("ha")
    block = lax.axis_index("az")
    place = block * n_ha + slab
    gathered = lax.all_gather(jnp.stack([profile_pick, terrain]), "az", axis=1, tiled=True)
    field, gathered = lax.optimization_barrier((field, gathered))
    both = ("az", "ha")
    h_dev, a_dev = field.shape[1], field.shape[2]
    total_h, total_a = h_dev * n_ha, a_dev * n_az
    cols = a_dev // n_ha
    bottom = clutter_mask.shape[0]
    h_first = max(64, n_dev)
    h_second = total_h // h_first
    own = h_first // n_dev
    lanes = 128 if cols % 128 == 0 else cols
    chunks = cols // lanes
    n_prof = profile_table.shape[0]

    taps_range = pulse.shape[0]
    half_range = (taps_range - 1) // 2
    half_beam = (beam.shape[0] - 1) // 2
    reach = 2 * half_beam
    wide = a_dev + 2 * reach
    middle = a_dev + 2 * half_beam
    share = bottom // n_ha
    rmat = band(pulse, iota((bottom, bottom), 1) - iota((bottom, bottom), 0) + half_range)
    forward_band = band(beam, iota((wide, middle), 0) - iota((wide, middle), 1))
    back_band = band(beam, iota((middle, a_dev), 1) - iota((middle, a_dev), 0) + reach)
    own_rmat = lax.dynamic_slice_in_dim(rmat, slab * share, share, 1)
    mask = clutter_mask.astype(jnp.float32)
    left, right = halo(mask, reach)
    wide_mask = jnp.concatenate([left, mask, right], axis=1)
    left, right = halo(measured, half_beam)
    wide_measured = jnp.concatenate([left, measured, right], axis=2)

    def sources_of(strip, step):
        strip = jnp.concatenate(ha_order(ha_trade(lambda to: strip)), axis=2)
        left, right = halo(strip, reach)
        strip = jnp.concatenate([left, strip, right], axis=2)
        low_re, low_im = strip[0], strip[1]
        power = wide_mask * (low_re * low_re + low_im * low_im)
        ranged = jnp.dot(rmat, power, precision=EXACT)
        misfit = jnp.dot(ranged, forward_band, precision=EXACT) - wide_measured[step]
        spread_back = jnp.dot(misfit, back_band, precision=EXACT)
        back = jnp.einsum("pr,pa->ra", own_rmat, spread_back, precision=EXACT)
        weight = 2.0 * lax.dynamic_slice_in_dim(mask, slab * share, share, 0) * back
        mine = [
            lax.dynamic_slice(low, (slab * share, reach), (share, a_dev)) for low in (low_re, low_im)
        ]
        return jnp.stack([weight * mine[0], weight * mine[1]])

    all_pick, all_terrain = gathered[0], gathered[1]
    height = iota((1, total_h), 1)
    z_chirp = chirp(height, height_chirp, total_h)
    z_gain = gauss(height_chirp, total_h)
    y_gain = gauss(azimuth_chirp, total_a)
    gain = (z_gain[0] * y_gain[0] - z_gain[1] * y_gain[1], z_gain[0] * y_gain[1] + z_gain[1] * y_gain[0])
    amount = damping(height, total_h)
    bend = cmul((amount * jnp.cos(profile_table), amount * jnp.sin(profile_table)), cmul(z_chirp, gain))
    bend_again = cmul(bend, z_chirp)
    slab_z = chirp(slab * h_dev + iota((h_dev, 1), 0), height_chirp, total_h)
    block_y = chirp(block * a_dev + iota((1, a_dev), 1), azimuth_chirp, total_a)
    w_first = roots(h_first, height_chirp, total_h)
    w_second = roots(h_second, height_chirp, total_h)
    w_in = w_first.reshape(2, 2, h_first, n_ha, h_first // n_ha)
    tw_re, tw_im = (t[:, :, None] for t in twist(h_first, h_second, height_chirp, total_h))
    w_blocks = roots(n_dev, azimuth_chirp, total_a)
    w_cols = roots(cols, azimuth_chirp, total_a)
    ty_re, ty_im = (t[:, None, None, :] for t in twist(n_dev, cols, azimuth_chirp, total_a))

    def send_chunk(chunk):
        def piece_for(to):
            def columns(cells):
                return choose(
                    [cells[..., i * cols + chunk * lanes:][..., :lanes] for i in range(n_ha)], to
                )

            y_part = (columns(block_y[0]), columns(block_y[1]))
            return jnp.stack(cmul((columns(field[0]), columns(field[1])), cmul(slab_z, y_part)))

        return ha_trade(piece_for)

    def to_rows(parts):
        tall = 0.0
        for shift, part in enumerate(parts):
            part = part.reshape(2, h_first // n_ha, h_second, lanes)
            w_part = lax.dynamic_index_in_dim(w_in, (slab - shift) % n_ha, 3, False)
            tall = tall + jnp.einsum("ocka,cabq->okbq", w_part, part, precision=FAST)
        tall = jnp.stack(cmul(tall, (tw_re, tw_im)))
        tall = jnp.einsum("ocjb,ckbq->kojq", w_second, tall, precision=FAST)
        tall = tall.reshape(n_dev, own, 2, h_second, lanes)
        return lax.all_to_all(tall, both, split_axis=0, concat_axis=0)

    sent = [send_chunk(chunk) for chunk in range(chunks)]
    arrived = [to_rows(parts) for parts in sent]
    rows = 0.0
    for chunk, part in enumerate(arrived):
        span = slice(chunk * lanes, (chunk + 1) * lanes)
        part = jnp.einsum("ocnp,pucjq->onujq", w_blocks, part, precision=FAST)
        part = jnp.stack(cmul(part, (ty_re[..., span], ty_im[..., span])))
        rows = rows + jnp.einsum("ocmq,cnujq->onujm", w_cols[..., span], part, precision=FAST)

    def own_rows(table):
        table = table.reshape(n_prof, h_second, n_dev, own)
        table = lax.dynamic_slice_in_dim(table, place, 1, 2)[:, :, 0]
        return jnp.swapaxes(table, 1, 2)

    own_first = place * own + iota((1, own, 1, 1), 1)
    own_height = own_first + h_first * iota((1, 1, h_second, 1), 2)
    grid_pick = all_pick.reshape(cols, n_dev).T
    grid_terrain = all_terrain.reshape(cols, n_dev).T
    hot = onehot_of(grid_pick, n_prof)
    azimuth = iota((n_dev, cols), 0) + n_dev * iota((n_dev, cols), 1)
    y_chirp = chirp(azimuth, azimuth_chirp, total_a)
    ground = (own_height >= grid_terrain[:, None, None, :]).astype(jnp.float32)
    y_turn = tuple(t[:, None, None, :] for t in cmul(y_chirp, y_chirp))
    bent = tuple(
        ground * jnp.einsum("fuj,fnm->nujm", own_rows(t), hot, precision=FAST) for t in bend_again
    )
    next_rows = jnp.stack(cmul(rows, cmul(bent, y_turn)))

    def to_tall(chunk):
        span = slice(chunk * lanes, (chunk + 1) * lanes)
        part = jnp.einsum("ocqm,cnujm->onujq", w_cols[:, :, span], next_rows, precision=FAST)
        part = jnp.stack(cmul(part, (ty_re[..., span], ty_im[..., span])))
        part = jnp.einsum("ocpn,cnujq->puojq", w_blocks, part, precision=FAST)
        return lax.all_to_all(part, both, split_axis=0, concat_axis=0)

    returned = [to_tall(chunk) for chunk in range(chunks)]

    n_low = -(-bottom // h_first)
    low_bend = tuple(
        ground[:, :, :n_low]
        * jnp.einsum("fuj,fnm->nujm", own_rows(t)[:, :, :n_low], hot, precision=EXACT)
        for t in bend
    )
    low_chirp = tuple(t[:, None, None, :] for t in y_chirp)
    low = jnp.stack(cmul(rows[:, :, :, :n_low], cmul(low_bend, low_chirp)))
    low = low.transpose(0, 2, 3, 4, 1).reshape(2, own, n_low, n_dev, cols)
    low = lax.all_to_all(low.transpose(3, 0, 1, 2, 4), both, split_axis=0, concat_axis=0)
    low = low.transpose(1, 3, 0, 2, 4).reshape(2, n_low * h_first, cols)[:, :bottom]
    first_sources = sources_of(low, 0)

    lasts = []
    outs = []
    for chunk, part in enumerate(returned):
        part = part.reshape(h_first, 2, h_second, lanes)
        part = jnp.einsum("ocbj,kcjq->okbq", w_second, part, precision=FAST)
        part = jnp.stack(cmul(part, (tw_re, tw_im)))
        part = jnp.einsum("ocak,ckbq->oabq", w_first, part, precision=FAST)
        part = part.reshape(2, total_h, lanes)
        col_start = slab * cols + chunk * lanes
        tall_pick = lax.dynamic_slice_in_dim(profile_pick, col_start, lanes, 0)
        tall_terrain = lax.dynamic_slice_in_dim(terrain, col_start, lanes, 0)
        tall_hot = onehot_of(tall_pick, n_prof)
        tall_ground = (iota((total_h, 1), 0) >= tall_terrain[None, :]).astype(jnp.float32)
        tall_y = chirp(block * a_dev + col_start + iota((1, lanes), 1), azimuth_chirp, total_a)
        tall_bent = tuple(
            tall_ground * jnp.einsum("fh,fq->hq", t, tall_hot, precision=FAST) for t in bend
        )
        last = jnp.stack(cmul(part, cmul(tall_bent, tall_y)))
        lasts.append(last)
        outs.append(
            ha_order(ha_trade(lambda to: lax.dynamic_slice_in_dim(last, to * h_dev, h_dev, 1)))
        )
    strip = jnp.concatenate([last[:, :bottom] for last in lasts], axis=2)
    second_sources = sources_of(strip, 1)
    out = jnp.concatenate([outs[j][i] for i in range(n_ha) for j in range(chunks)], axis=2)
    return (out, jnp.stack([first_sources, second_sources]))


def solution(mesh):
    return jax.shard_map(
        local,
        mesh=mesh,
        in_specs=(
            P(None, "ha", "az"),
            P("az"),
            P("az"),
            P(),
            P(None, "az"),
            P(),
            P(),
            P(None, None, "az"),
        ),
        out_specs=(P(None, "ha", "az"), P(None, None, "ha", "az")),
        check_vma=False,
    )
```

```python
import math

import jax
import jax.numpy as jnp
import numpy as np
from jax import lax
from jax.experimental.layout import Layout, with_layout_constraint
from jax.sharding import PartitionSpec as P

height_chirp = 1
azimuth_chirp = 3
EXACT = lax.Precision.HIGHEST
FAST = lax.Precision.HIGH


def iota(shape, dim):
    return lax.broadcasted_iota(jnp.int32, shape, dim)


def cmul(left, right):
    return (left[0] * right[0] - left[1] * right[1], left[0] * right[1] + left[1] * right[0])


def turn(amount, period, scale=1.0):
    angle = (amount % period).astype(jnp.float32) * (2.0 * math.pi / period)
    return (scale * jnp.cos(angle), scale * jnp.sin(angle))


def inverse_of(spread, count):
    return pow(spread, -1, 2 * count)


def gauss(spread, count):
    index = np.arange(count, dtype=np.int64)
    angle = (spread * index * index % (2 * count)) * (-math.pi / count)
    return (float(np.sum(np.cos(angle))) / count, float(np.sum(np.sin(angle))) / count)


def chirp(index, spread, count):
    return turn(index * index % (2 * count) * inverse_of(spread, count), 2 * count)


def roots(size, spread, count):
    amount = iota((size, size), 0) * iota((size, size), 1) % size * (inverse_of(spread, count) % size)
    re, im = turn(-amount, size)
    return jnp.stack([jnp.stack([re, -im]), jnp.stack([im, re])])


def twist(rows, cols, spread, count):
    left, right = iota((rows, cols), 0), iota((rows, cols), 1)
    return turn(-(left * right % count * (inverse_of(spread, count) % count)), count)


def band(taps, offset):
    hit = offset[:, :, None] == lax.broadcasted_iota(jnp.int32, (1, 1, taps.shape[0]), 2)
    return jnp.sum(jnp.where(hit, taps[None, None, :], 0.0), axis=-1)


def damping(rows, total):
    depth = jnp.maximum(rows.astype(jnp.float32) - 0.75 * total, 0.0) / (0.25 * total)
    return jnp.exp(-4.0 * depth * depth)


def onehot_of(picks, count):
    return (picks[None] == iota((count,) + picks.shape, 0)).astype(jnp.float32)


def halo(cells, width, axis="az"):
    count = lax.axis_size(axis)
    head = cells[..., :width]
    tail = cells[..., cells.shape[-1] - width:]
    left = lax.ppermute(tail, axis, [(i, (i + 1) % count) for i in range(count)])
    right = lax.ppermute(head, axis, [((i + 1) % count, i) for i in range(count)])
    return left, right


def choose(options, index):
    picked = options[0]
    for i in range(1, len(options)):
        picked = jnp.where(index == i, options[i], picked)
    return picked


def ha_trade(piece_for):
    count = lax.axis_size("ha")
    slab = lax.axis_index("ha")
    parts = [piece_for(slab)]
    for shift in range(1, count):
        pairs = [(i, (i + shift) % count) for i in range(count)]
        parts.append(lax.ppermute(piece_for((slab + shift) % count), "ha", pairs))
    return parts


def ha_order(parts):
    count = len(parts)
    slab = lax.axis_index("ha")
    return [choose(parts, (slab - source) % count) for source in range(count)]


def local(field, terrain, profile_pick, profile_table, clutter_mask, pulse, beam, measured):
    n_ha = lax.axis_size("ha")
    n_az = lax.axis_size("az")
    n_dev = n_ha * n_az
    slab = lax.axis_index("ha")
    block = lax.axis_index("az")
    place = block * n_ha + slab
    gathered = lax.all_gather(jnp.stack([profile_pick, terrain]), "az", axis=1, tiled=True)
    field, gathered = lax.optimization_barrier((field, gathered))
    both = ("az", "ha")
    h_dev, a_dev = field.shape[1], field.shape[2]
    total_h, total_a = h_dev * n_ha, a_dev * n_az
    cols = a_dev // n_ha
    bottom = clutter_mask.shape[0]
    h_first = max(64, n_dev)
    h_second = total_h // h_first
    own = h_first // n_dev
    lanes = 128 if cols % 128 == 0 else cols
    chunks = cols // lanes
    n_prof = profile_table.shape[0]

    taps_range = pulse.shape[0]
    half_range = (taps_range - 1) // 2
    half_beam = (beam.shape[0] - 1) // 2
    reach = 2 * half_beam
    wide = a_dev + 2 * reach
    middle = a_dev + 2 * half_beam
    share = bottom // n_ha
    rmat = band(pulse, iota((bottom, bottom), 1) - iota((bottom, bottom), 0) + half_range)
    forward_band = band(beam, iota((wide, middle), 0) - iota((wide, middle), 1))
    back_band = band(beam, iota((middle, a_dev), 1) - iota((middle, a_dev), 0) + reach)
    own_rmat = lax.dynamic_slice_in_dim(rmat, slab * share, share, 1)
    mask = clutter_mask.astype(jnp.float32)
    left, right = halo(mask, reach)
    wide_mask = jnp.concatenate([left, mask, right], axis=1)
    left, right = halo(measured, half_beam)
    wide_measured = jnp.concatenate([left, measured, right], axis=2)

    def sources_of(strips):
        strips = jnp.concatenate(ha_order(ha_trade(lambda to: strips)), axis=3)
        left, right = halo(strips, reach)
        strips = jnp.concatenate([left, strips, right], axis=3)
        result = []
        for step in range(strips.shape[0]):
            low_re, low_im = strips[step, 0], strips[step, 1]
            power = wide_mask * (low_re * low_re + low_im * low_im)
            ranged = jnp.dot(rmat, power, precision=EXACT)
            misfit = jnp.dot(ranged, forward_band, precision=EXACT) - wide_measured[step]
            spread_back = jnp.dot(misfit, back_band, precision=EXACT)
            back = jnp.einsum("pr,pa->ra", own_rmat, spread_back, precision=EXACT)
            weight = 2.0 * lax.dynamic_slice_in_dim(mask, slab * share, share, 0) * back
            mine = [
                lax.dynamic_slice(low, (slab * share, reach), (share, a_dev))
                for low in (low_re, low_im)
            ]
            result.append(jnp.stack([weight * mine[0], weight * mine[1]]))
        return jnp.stack(result)

    all_pick, all_terrain = gathered[0], gathered[1]
    height = iota((1, total_h), 1)
    z_chirp = chirp(height, height_chirp, total_h)
    z_gain = gauss(height_chirp, total_h)
    y_gain = gauss(azimuth_chirp, total_a)
    gain = (z_gain[0] * y_gain[0] - z_gain[1] * y_gain[1], z_gain[0] * y_gain[1] + z_gain[1] * y_gain[0])
    amount = damping(height, total_h)
    bend = cmul((amount * jnp.cos(profile_table), amount * jnp.sin(profile_table)), cmul(z_chirp, gain))
    bend_again = cmul(bend, z_chirp)
    slab_z = chirp(slab * h_dev + iota((h_dev, 1), 0), height_chirp, total_h)
    block_y = chirp(block * a_dev + iota((1, a_dev), 1), azimuth_chirp, total_a)
    w_first = roots(h_first, height_chirp, total_h)
    w_second = roots(h_second, height_chirp, total_h)
    w_in = w_first.reshape(2, 2, h_first, n_ha, h_first // n_ha)
    tw_re, tw_im = (t[:, :, None] for t in twist(h_first, h_second, height_chirp, total_h))
    w_blocks = roots(n_dev, azimuth_chirp, total_a)
    w_cols = roots(cols, azimuth_chirp, total_a)
    ty_re, ty_im = (t[:, None, None, :] for t in twist(n_dev, cols, azimuth_chirp, total_a))

    def send_chunk(chunk):
        def piece_for(to):
            def columns(cells):
                return choose(
                    [cells[..., i * cols + chunk * lanes:][..., :lanes] for i in range(n_ha)], to
                )

            y_part = (columns(block_y[0]), columns(block_y[1]))
            return jnp.stack(cmul((columns(field[0]), columns(field[1])), cmul(slab_z, y_part)))

        return ha_trade(piece_for)

    def to_rows(parts):
        tall = 0.0
        for shift, part in enumerate(parts):
            part = part.reshape(2, h_first // n_ha, h_second, lanes)
            w_part = lax.dynamic_index_in_dim(w_in, (slab - shift) % n_ha, 3, False)
            tall = tall + jnp.einsum("ocka,cabq->okbq", w_part, part, precision=FAST)
        tall, tw = lax.optimization_barrier((tall, (tw_re, tw_im)))
        tall = jnp.stack(cmul(tall, tw))
        tall = jnp.einsum("ocjb,ckbq->kojq", w_second, tall, precision=FAST)
        return tall.reshape(n_dev, own * 2 * h_second, lanes)

    sent = [send_chunk(chunk) for chunk in range(chunks)]
    arrived = []
    for chunk, parts in enumerate(sent):
        if chunk > 0:
            parts, _ = lax.optimization_barrier((parts, tall))
        tall = to_rows(parts)
        arrived.append(lax.all_to_all(tall, both, split_axis=0, concat_axis=0))
    rows = 0.0
    for chunk, part in enumerate(arrived):
        span = slice(chunk * lanes, (chunk + 1) * lanes)
        part = part.reshape(n_dev, own, 2, h_second, lanes)
        part = jnp.einsum("ocnp,pucjq->onujq", w_blocks, part, precision=FAST)
        part, ty = lax.optimization_barrier((part, (ty_re[..., span], ty_im[..., span])))
        part = jnp.stack(cmul(part, ty))
        rows = rows + jnp.einsum("ocmq,cnujq->onujm", w_cols[..., span], part, precision=FAST)

    def own_rows(table):
        table = table.reshape(n_prof, h_second, n_dev, own)
        table = lax.dynamic_slice_in_dim(table, place, 1, 2)[:, :, 0]
        return jnp.swapaxes(table, 1, 2)

    own_first = place * own + iota((1, own, 1, 1), 1)
    own_height = own_first + h_first * iota((1, 1, h_second, 1), 2)
    grid_pick = all_pick.reshape(cols, n_dev).T
    grid_terrain = all_terrain.reshape(cols, n_dev).T
    hot = onehot_of(grid_pick, n_prof)
    azimuth = iota((n_dev, cols), 0) + n_dev * iota((n_dev, cols), 1)
    y_chirp = chirp(azimuth, azimuth_chirp, total_a)
    ground = (own_height >= grid_terrain[:, None, None, :]).astype(jnp.float32)
    y_turn = tuple(t[:, None, None, :] for t in cmul(y_chirp, y_chirp))
    bent = tuple(
        ground * jnp.einsum("fuj,fnm->nujm", own_rows(t), hot, precision=FAST) for t in bend_again
    )
    next_rows = jnp.stack(cmul(rows, cmul(bent, y_turn)))

    def to_tall(chunk, cells):
        span = slice(chunk * lanes, (chunk + 1) * lanes)
        part = jnp.einsum("ocqm,cnujm->onujq", w_cols[:, :, span], cells, precision=FAST)
        part, ty = lax.optimization_barrier((part, (ty_re[..., span], ty_im[..., span])))
        part = jnp.stack(cmul(part, ty))
        part = jnp.einsum("ocpn,cnujq->puojq", w_blocks, part, precision=FAST)
        return part.reshape(n_dev, own * 2 * h_second, lanes)

    returned = []
    for chunk in range(chunks):
        if chunk > 0:
            next_rows, _ = lax.optimization_barrier((next_rows, part))
        part = to_tall(chunk, next_rows)
        returned.append(lax.all_to_all(part, both, split_axis=0, concat_axis=0))

    n_low = -(-bottom // h_first)
    low_bend = tuple(
        ground[:, :, :n_low]
        * jnp.einsum("fuj,fnm->nujm", own_rows(t)[:, :, :n_low], hot, precision=EXACT)
        for t in bend
    )
    low_chirp = tuple(t[:, None, None, :] for t in y_chirp)
    low = jnp.stack(cmul(rows[:, :, :, :n_low], cmul(low_bend, low_chirp)))
    low = low.transpose(0, 2, 3, 4, 1).reshape(2, own, n_low, n_dev, cols)
    low = lax.all_to_all(low.transpose(3, 0, 1, 2, 4), both, split_axis=0, concat_axis=0)
    low = low.transpose(1, 3, 0, 2, 4).reshape(2, n_low * h_first, cols)[:, :bottom]

    lasts = []
    outs = []
    for chunk, part in enumerate(returned):
        if lasts:
            part, _ = lax.optimization_barrier((part, lasts[-1]))
        part = part.reshape(h_first, 2, h_second, lanes)
        part = jnp.einsum("ocbj,kcjq->okbq", w_second, part, precision=FAST)
        part, tw = lax.optimization_barrier((part, (tw_re, tw_im)))
        part = jnp.stack(cmul(part, tw))
        part = jnp.einsum("ocak,ckbq->oabq", w_first, part, precision=FAST)
        part = part.reshape(2, total_h, lanes)
        col_start = slab * cols + chunk * lanes
        tall_pick = lax.dynamic_slice_in_dim(profile_pick, col_start, lanes, 0)
        tall_terrain = lax.dynamic_slice_in_dim(terrain, col_start, lanes, 0)
        tall_hot = onehot_of(tall_pick, n_prof)
        tall_ground = (iota((total_h, 1), 0) >= tall_terrain[None, :]).astype(jnp.float32)
        tall_y = chirp(block * a_dev + col_start + iota((1, lanes), 1), azimuth_chirp, total_a)
        tall_bent = tuple(
            tall_ground * jnp.einsum("fh,fq->hq", t, tall_hot, precision=FAST) for t in bend
        )
        tall_bent = tuple(with_layout_constraint(t, Layout((0, 1))) for t in tall_bent)
        last = jnp.stack(cmul(part, cmul(tall_bent, tall_y)))
        last = with_layout_constraint(last, Layout((0, 1, 2)))
        lasts.append(last)
        outs.append(
            ha_order(ha_trade(lambda to: lax.dynamic_slice_in_dim(last, to * h_dev, h_dev, 1)))
        )
    strip = jnp.concatenate([last[:, :bottom] for last in lasts], axis=2)
    sources = sources_of(jnp.stack([low, strip]))
    out = jnp.concatenate([outs[j][i] for i in range(n_ha) for j in range(chunks)], axis=2)
    return (out, sources)


def solution(mesh):
    return jax.shard_map(
        local,
        mesh=mesh,
        in_specs=(
            P(None, "ha", "az"),
            P("az"),
            P("az"),
            P(),
            P(None, "az"),
            P(),
            P(),
            P(None, None, "az"),
        ),
        out_specs=(P(None, "ha", "az"), P(None, None, "ha", "az")),
        check_vma=False,
    )
```
